128 devices in a mesh: pts: 16 (over y, z), var: 8 (over x, core).
Axes of the slice: x: 4, y: 4, z: 4, core: 2. Of those that a mesh axis runs over, the one named last changes fastest.
Arguments:
- tensor: bfloat16 [8, 16384, 8192], P(None, 'pts', 'var'), may hold values from -36 to 36
- level_init: float32 [64, 8192], P(None, 'var'), may hold values from -6 to 6
- time_init: float32 [8, 64], replicated, may hold values from -6 to 6
Outputs:
- point_factor: float32 [64, 16384], P(None, 'pts')
- level_factor: float32 [64, 8192], P(None, 'var')
- time_out: float32 [8, 64], replicated
The draws below stay inside these ranges and needn't reach their ends.
All inputs are finite; a program needn't handle non-finite values.
Results may differ from the reference program's by a relative error of at most 0.011.
Values sent between devices are 32-bit elements; how exact they have to be, the bound alone decides.
A program may use at most 128 MiB of HBM per device.

```python
import math
import jax
import jax.numpy as jnp
from jax import lax

RANK = 64
STEPS = 8
SWEEPS = 3
POINTS = 16384
LEVELS = 8192


def draw_tensor(key, part):
    key_base, key_rows, key_cols = jax.random.split(key, 3)
    row_scale = jnp.exp(jax.random.uniform(key_rows, (1, POINTS, 1), jnp.float32, math.log(0.3), math.log(3.0)))
    col_scale = jnp.exp(jax.random.uniform(key_cols, (1, 1, LEVELS), jnp.float32, math.log(0.3), math.log(3.0)))
    base_vals = jnp.clip(jax.random.normal(key_base, (STEPS, POINTS, LEVELS), jnp.float32), -4.0, 4.0)
    return (base_vals * row_scale * col_scale).astype(jnp.bfloat16)


def block_scale(key, shape, cuts, least, top_value):
    gain, own = 1.0, jax.random.fold_in(key, 6)
    for dim, blocks in cuts:
        draws = jnp.exp(jax.random.uniform(jax.random.fold_in(own, dim), (blocks,), jnp.float32, least / len(cuts), top_value / len(cuts)))
        gain = gain * jnp.repeat(draws, shape[dim] // blocks).reshape([-1 if axis == dim else 1 for axis in range(len(shape))])
    return gain


def bell_draw(stream_key, extent, deviation, most, cuts=(), kind=jnp.bfloat16):
    level = block_scale(stream_key, extent, cuts, -0.22, 0.18) if cuts else 1.0
    entries = jax.random.normal(stream_key, extent, jnp.float32) * deviation * level
    return jnp.minimum(jnp.maximum(entries, -most), most).astype(kind)


def setup_inputs(seed: int = 0) -> dict:
    splits = jax.random.split(jax.random.key(seed), 4)
    tensor = draw_tensor(jax.random.fold_in(splits[3], 71), 0)
    level_init = bell_draw(splits[1], (RANK, LEVELS), 1.0, 6.0, ((1, 8),), jnp.float32)
    time_init = bell_draw(splits[2], (STEPS, RANK), 1.0, 6.0, (), jnp.float32)
    return dict(tensor=tensor, level_init=level_init, time_init=time_init)


HIGH_PRECISION = lax.Precision.HIGHEST
EPSILON = 1e-06

def gram_of(factor):
    return jnp.dot(factor.astype(jnp.float32), factor.T.astype(jnp.float32), precision=HIGH_PRECISION, preferred_element_type=jnp.float32)

def ridge_solve(gram_mat, right_side):
    order_count = gram_mat.shape[0]
    ridge_term = 0.01 * jnp.trace(gram_mat) / order_count + EPSILON
    system = gram_mat + ridge_term * jnp.eye(order_count, dtype=jnp.float32)
    chol_lower = jnp.linalg.cholesky(system)
    middle = lax.linalg.triangular_solve(chol_lower, right_side, left_side=True, lower=True)
    return lax.linalg.triangular_solve(chol_lower, middle, left_side=True, lower=True, transpose_a=True)

def unit_rows(factor, count):
    col_sumsq = lax.optimization_barrier(jnp.sum(factor * factor, axis=1))
    col_scale = 1.0 / jnp.sqrt(col_sumsq / count + EPSILON)
    return factor * col_scale[:, None]

def reference(tensor, level_init, time_init):
    level_factor = level_init
    level_grammat = gram_of(level_init)
    time_factor = time_init
    point_factor = None
    for sweep_index in range(SWEEPS):
        time_gram = jnp.dot(time_factor.T.astype(jnp.float32), time_factor.astype(jnp.float32), precision=HIGH_PRECISION, preferred_element_type=jnp.float32)
        level_bf = level_factor.astype(jnp.bfloat16)
        mttk_point = jnp.zeros((RANK, POINTS), jnp.float32)
        for step_index in range(STEPS):
            product = jnp.einsum('rv,pv->rp', level_bf.astype(jnp.float32), tensor[step_index].astype(jnp.float32), preferred_element_type=jnp.float32)
            mttk_point = mttk_point + time_factor[step_index][:, None] * product
        point_factor = unit_rows(ridge_solve(level_grammat * time_gram, mttk_point), POINTS)
        point_grammat = gram_of(point_factor)
        point_bf = point_factor.astype(jnp.bfloat16)
        mttk_level = jnp.zeros((RANK, LEVELS), jnp.float32)
        contracted = []
        for step_index in range(STEPS):
            product = jnp.dot(point_bf.astype(jnp.float32), tensor[step_index].astype(jnp.float32), preferred_element_type=jnp.float32)
            contracted.append(product)
            mttk_level = mttk_level + time_factor[step_index][:, None] * product
        level_factor = unit_rows(ridge_solve(point_grammat * time_gram, mttk_level), LEVELS)
        level_grammat = gram_of(level_factor)
        mttk_time = jnp.stack([lax.optimization_barrier(jnp.sum(product * level_factor, axis=1)) for product in contracted])
        time_factor = ridge_solve(point_grammat * level_grammat, mttk_time.T).T
    return (point_factor, level_factor, time_factor * math.sqrt(POINTS * LEVELS))
```

```python
import math

import jax
import jax.numpy as jnp
from jax import lax
from jax.experimental import pallas as pl
from jax.experimental.pallas import tpu as pltpu
from jax.sharding import PartitionSpec as P

RANK = 64
STEPS = 8
SWEEPS = 3
NY = NZ = NX = 4
PTS_DEVICES = NY * NZ
CHIPS = PTS_DEVICES * NX
EPSILON = 1e-06
F32 = jnp.float32
BF16 = jnp.bfloat16
HIGHEST = lax.Precision.HIGHEST
MESH = pl.DeviceIdType.MESH


def spd_inverse(matrix, block=8):
    n = RANK
    shape = (8, n)
    row_ids = lax.broadcasted_iota(jnp.int32, shape, 0)
    lane_ids = lax.broadcasted_iota(jnp.int32, shape, 1)
    tiles = [matrix[8 * i : 8 * i + 8, :] for i in range(n // 8)]
    for start in range(0, n, block):
        panel = {
            j: [jnp.broadcast_to(tile[:, j : j + 1], shape) for tile in tiles]
            for j in range(start, start + block)
        }
        for k in range(start, start + block):
            t, s = divmod(k, 8)
            inv_pivot = 1.0 / jnp.broadcast_to(panel[k][t][s : s + 1, :], shape)
            col = list(panel[k])
            col[t] = jnp.where(row_ids == s, -1.0, col[t])
            for j in range(k + 1, start + block):
                scaled = jnp.broadcast_to(panel[j][t][s : s + 1, :], shape) * inv_pivot
                new = [panel[j][i] - col[i] * scaled for i in range(n // 8)]
                new[t] = jnp.where(row_ids == s, scaled, new[t])
                panel[j] = new
            row = jnp.broadcast_to(tiles[t][s : s + 1, :], shape) * inv_pivot
            row = jnp.where(lane_ids == k, inv_pivot, row)
            base = [jnp.where(lane_ids == k, 0.0, tile) for tile in tiles]
            base[t] = jnp.where(row_ids == s, 0.0, base[t])
            tiles = [base[i] - col[i] * row for i in range(n // 8)]
    return jnp.concatenate(tiles, axis=0)


def eye_mask():
    rows = lax.broadcasted_iota(jnp.int32, (RANK, RANK), 0)
    cols = lax.broadcasted_iota(jnp.int32, (RANK, RANK), 1)
    return rows == cols


def ridge_inverse(gram):
    eye = eye_mask()
    trace = jnp.sum(
        jnp.sum(jnp.where(eye, gram, 0.0), axis=0, keepdims=True), axis=1, keepdims=True
    )
    ridge = 0.01 * trace / RANK + EPSILON
    return spd_inverse(gram + jnp.where(eye, ridge, 0.0))


def packed_gram(factor):
    high = factor.astype(BF16)
    low = (factor - high.astype(F32)).astype(BF16)
    both = jnp.concatenate([high, low], axis=0)
    g = lax.dot_general(both, both, (((1,), (1,)), ((), ())), preferred_element_type=F32)
    rows = g[:RANK] + g[RANK:]
    gram = rows[:, :RANK] + rows[:, RANK:]
    return jnp.concatenate([gram[:32], gram[32:]], axis=1)


def unpacked(folded):
    return jnp.concatenate([folded[:, :RANK], folded[:, RANK:]], axis=0)


def unit_scales(gram, count):
    diag = jnp.where(eye_mask(), gram, 0.0)
    col = 1.0 / jnp.sqrt(jnp.sum(diag, axis=1, keepdims=True) / count + EPSILON)
    row = 1.0 / jnp.sqrt(jnp.sum(diag, axis=0, keepdims=True) / count + EPSILON)
    return col, row


def sweeps_kernel(
    points_all,
    levels_all,
    x_hbm,
    level_ref,
    time_ref,
    point_out,
    level_out,
    time_out,
    x_ref,
    y_ref,
    c_ref,
    lbf_ref,
    pbf_ref,
    lu_ref,
    pu_ref,
    gl_ref,
    gp_ref,
    tt_ref,
    tr_ref,
    slcol_ref,
    mp_ref,
    sib_mp,
    rs_mp,
    m_full,
    g_send,
    g_recv,
    gh_full,
    ml_send,
    ml_recv,
    ml_full,
    gl_send,
    gl_sib,
    gl_x,
    t_send,
    t_sib,
    t_all,
    x_sem,
    send_sems,
    mp_sem,
    rs_sem,
    ag_sem,
    fw_sem,
    g_sem,
    gs_sem,
    ml_sem,
    la_sem,
    gls_sem,
    glx_sem,
    ts_sem,
    ta_sem,
):
    pts, var = lax.axis_index("pts"), lax.axis_index("var")
    y, z = lax.div(pts, NZ), lax.rem(pts, NZ)
    x, core = lax.div(var, 2), lax.rem(var, 2)
    other = 1 - core
    sibling = (pts, x * 2 + other)
    chip = pts * NX + x

    def x_peer(d):
        return lax.rem(x + d, NX)

    def send(src, dst, send_sem, recv_sem, device):
        copy = pltpu.make_async_remote_copy(
            src_ref=src,
            dst_ref=dst,
            send_sem=send_sem,
            recv_sem=recv_sem,
            device_id=device,
            device_id_type=MESH,
        )
        copy.start()
        return copy

    def wait_bytes(ref, sem):
        pltpu.make_async_copy(ref, ref, sem).wait()

    loads = [pltpu.make_async_copy(x_hbm.at[k], x_ref.at[k], x_sem.at[k]) for k in range(STEPS)]
    for load in loads:
        load.start()
    barrier = pltpu.get_barrier_semaphore()
    pl.semaphore_signal(barrier, inc=1, device_id=sibling, device_id_type=MESH)

    def chip_device(d):
        target = lax.rem(chip + d, CHIPS)
        return (lax.div(target, NX), lax.rem(target, NX) * 2 + core)

    def greet(d, carry):
        pl.semaphore_signal(barrier, inc=1, device_id=chip_device(d), device_id_type=MESH)
        return carry

    lax.fori_loop(1, CHIPS, greet, 0)

    def pass_levels(k):
        y_ref[k] = lax.dot_general(
            lbf_ref[...], x_ref[k], (((1,), (1,)), ((), ())), preferred_element_type=F32
        )

    def level_gram_start(slot):
        gl_send[...] = packed_gram(lu_ref[...])
        return send(gl_send, gl_sib.at[slot], send_sems.at[0], gls_sem.at[slot], sibling)

    def level_gram_middle(slot, copy):
        copy.wait()
        gl_x[slot, x] = gl_send[...] + gl_sib[slot]
        return [
            send(
                gl_x.at[slot, x],
                gl_x.at[slot, x],
                send_sems.at[d],
                glx_sem.at[slot, d],
                (pts, x_peer(d) * 2 + core),
            )
            for d in range(1, NX)
        ]

    def level_gram_end(slot, copies):
        for copy in copies:
            copy.wait()
        return unpacked(jnp.sum(gl_x[slot], axis=0))

    def column(values, k, lanes):
        return jnp.broadcast_to(values[:, k : k + 1], (values.shape[0], lanes))

    lu_ref[...] = level_ref[...]
    lbf_ref[...] = level_ref[...].astype(BF16)
    tr_ref[...] = time_ref[...]
    tt_ref[...] = lax.dot_general(
        jnp.where(eye_mask(), 1.0, 0.0),
        time_ref[...],
        (((1,), (1,)), ((), ())),
        precision=HIGHEST,
        preferred_element_type=F32,
    )
    slcol_ref[...] = jnp.ones_like(slcol_ref)
    pl.semaphore_wait(barrier, CHIPS)
    first = level_gram_start(0)
    loads[0].wait()
    pass_levels(0)
    second = level_gram_middle(0, first)
    for k in range(1, STEPS):
        loads[k].wait()
        pass_levels(k)
    gl_ref[...] = level_gram_end(0, second)

    share_points = y_ref.shape[2] // (2 * NX)
    quarter = c_ref.shape[2] // NY
    group = RANK // NZ

    def sweep(s, carry):
        time_cols = tt_ref[...]
        weights = time_cols * slcol_ref[...]
        spread = [column(weights, k, share_points) for k in range(STEPS)]

        def point_share(lane_start):
            total = spread[0] * y_ref[0, :, pl.ds(lane_start, share_points)]
            for k in range(1, STEPS):
                total += spread[k] * y_ref[k, :, pl.ds(lane_start, share_points)]
            return total

        def share_lanes(chip_x, c):
            return pl.multiple_of((chip_x * 2 + c) * share_points, share_points)

        for j in range(NX):
            mp_ref[0, j] = point_share(share_lanes(j, other))
        to_sibling = send(mp_ref.at[0], sib_mp.at[s], send_sems.at[0], mp_sem.at[s], sibling)
        for j in range(NX):
            mp_ref[1, j] = point_share(share_lanes(j, core))
        to_sibling.wait()
        for j in range(NX):
            mp_ref[1, j] += sib_mp[s, j]
        scatter = [
            send(
                mp_ref.at[1, x_peer(d)],
                rs_mp.at[s, d - 1],
                send_sems.at[d],
                rs_sem.at[s, d],
                (pts, x_peer(d) * 2 + core),
            )
            for d in range(1, NX)
        ]

        rows = tr_ref[...]
        time_gram = column(time_cols, 0, RANK) * rows[0:1, :]
        for k in range(1, STEPS):
            time_gram += column(time_cols, k, RANK) * rows[k : k + 1, :]
        inverse = ridge_inverse(gl_ref[...] * time_gram)

        for copy in scatter:
            copy.wait()
        own = mp_ref[1, x]
        for d in range(1, NX):
            own += rs_mp[s, d - 1]
        own_lanes = pl.ds(share_lanes(x, core), share_points)
        m_full[s, :, own_lanes] = own
        own_view = m_full.at[s, :, own_lanes]
        gather = [
            send(
                own_view,
                own_view,
                send_sems.at[d],
                ag_sem.at[s, d],
                (pts, x_peer(d) * 2 + core),
            )
            for d in range(1, NX)
        ]
        forward = [send(own_view, own_view, send_sems.at[0], fw_sem.at[s, 0], sibling)]
        for d in (1, 3, 2):
            gather[d - 1].wait()
            source = lax.rem(x + NX - d, NX)
            view = m_full.at[s, :, pl.ds(share_lanes(source, core), share_points)]
            forward.append(send(view, view, send_sems.at[NX + d], fw_sem.at[s, d], sibling))
        for copy in forward:
            copy.wait()

        solved = jnp.dot(inverse, m_full[s], precision=HIGHEST, preferred_element_type=F32)
        pu_ref[...] = solved
        pbf_ref[...] = solved.astype(BF16)

        g_send[...] = packed_gram(solved)
        half = pl.ds(pl.multiple_of(core * 16, 16), 16)
        g_recv[s, pts] = g_send[half, :]

        def pts_device(d):
            return (lax.rem(pts + d, PTS_DEVICES), var)

        for d in range(1, PTS_DEVICES):
            send(
                g_send.at[half, :],
                g_recv.at[s, pts],
                send_sems.at[0],
                g_sem.at[s],
                pts_device(d),
            )

        for dy in (2, 1, 3, 0):
            q = lax.rem(y + dy, NY)
            lanes = pl.ds(pl.multiple_of(q * quarter, quarter), quarter)
            total = None
            for k in range(STEPS):
                product = jnp.dot(pbf_ref[...], x_ref[k, :, lanes], preferred_element_type=F32)
                c_ref[k, :, lanes] = product
                term = column(time_cols, k, quarter) * product
                total = term if total is None else total + term
            for j in range(NZ):
                ml_send[q, j] = total[j * group : (j + 1) * group]
            for dz in (2, 1, 3, 0):
                if dy == 0 and dz == 0:
                    continue
                zz = lax.rem(z + dz, NZ)
                send(
                    ml_send.at[q, zz],
                    ml_recv.at[s, pts],
                    send_sems.at[1],
                    ml_sem.at[s],
                    (q * NZ + zz, var),
                )
        ml_recv[s, pts] = ml_send[y, z]

        others = pl.ds(0, PTS_DEVICES - 1)
        wait_bytes(g_recv.at[s, others], g_sem.at[s])
        wait_bytes(g_recv.at[s, others], send_sems.at[0])
        gh_full[s, half, :] = jnp.sum(g_recv[s], axis=0)
        half_view = gh_full.at[s, half, :]
        half_copy = send(half_view, half_view, send_sems.at[2], gs_sem.at[s], sibling)

        wait_bytes(ml_recv.at[s, others], ml_sem.at[s])
        wait_bytes(ml_recv.at[s, others], send_sems.at[1])
        own_rows = pl.ds(pl.multiple_of(z * group, group), group)
        own_cols = pl.ds(pl.multiple_of(y * quarter, quarter), quarter)
        ml_full[s, own_rows, own_cols] = jnp.sum(ml_recv[s], axis=0)
        level_view = ml_full.at[s, own_rows, own_cols]
        for d in range(1, PTS_DEVICES):
            send(level_view, level_view, send_sems.at[1], la_sem.at[s], pts_device(d))

        half_copy.wait()
        raw_gram = unpacked(gh_full[s])
        point_col, point_row = unit_scales(raw_gram, points_all)
        point_gram = point_col * raw_gram * point_row
        gp_ref[...] = point_gram
        inverse = ridge_inverse(point_gram * time_gram) * point_row
        point_out[...] = pu_ref[...] * point_col

        wait_bytes(ml_recv.at[s, others], la_sem.at[s])
        wait_bytes(ml_recv.at[s, others], send_sems.at[1])
        solved = jnp.dot(inverse, ml_full[s], precision=HIGHEST, preferred_element_type=F32)
        lu_ref[...] = solved
        lbf_ref[...] = solved.astype(BF16)
        scaled = solved * point_col

        lane_ids = lax.broadcasted_iota(jnp.int32, (RANK, 128), 1)
        products = jnp.zeros((RANK, 128), F32)
        for k in range(STEPS):
            sums = jnp.sum(c_ref[k] * scaled, axis=1, keepdims=True)
            products = jnp.where(lane_ids == k, sums, products)
        t_rows = jnp.transpose(products)[:STEPS]
        t_send[:, :RANK] = t_rows
        t_send[:, RANK:] = jnp.zeros_like(t_rows)
        time_copy = send(t_send, t_sib.at[s], send_sems.at[NX], ts_sem.at[s], sibling)
        first = level_gram_start(s + 1)
        time_copy.wait()
        t_all[s, chip] = t_send[...] + t_sib[s]

        def spread_time(d, carry):
            send(
                t_all.at[s, chip],
                t_all.at[s, chip],
                send_sems.at[NX + 1],
                ta_sem.at[s],
                chip_device(d),
            )
            return carry

        lax.fori_loop(1, CHIPS, spread_time, 0)
        second = level_gram_middle(s + 1, first)
        for k in range(STEPS):
            pass_levels(k)
        raw_gram = level_gram_end(s + 1, second)
        level_col, level_row = unit_scales(raw_gram, levels_all)
        level_gram = level_col * raw_gram * level_row
        gl_ref[...] = level_gram
        slcol_ref[...] = jnp.broadcast_to(level_col, slcol_ref.shape)
        inverse = ridge_inverse(gp_ref[...] * level_gram)
        level_out[...] = lu_ref[...] * level_col

        chips = pl.ds(0, CHIPS - 1)
        wait_bytes(t_all.at[s, chips], ta_sem.at[s])
        wait_bytes(t_all.at[s, chips], send_sems.at[NX + 1])
        mttk_time = jnp.sum(t_all[s], axis=0)[:, :RANK] * level_row
        tr_ref[...] = jnp.dot(mttk_time, inverse, precision=HIGHEST, preferred_element_type=F32)
        tt_ref[...] = lax.dot_general(
            inverse,
            mttk_time,
            (((1,), (1,)), ((), ())),
            precision=HIGHEST,
            preferred_element_type=F32,
        )
        return carry

    lax.fori_loop(0, SWEEPS, sweep, 0)
    time_out[...] = tr_ref[...] * math.sqrt(points_all * levels_all)


def solution(mesh):
    def per_device(tensor, level_init, time_init):
        steps, points, levels = tensor.shape
        points_all = points * mesh.shape["pts"]
        levels_all = levels * mesh.shape["var"]
        share = points // (2 * NX)
        group, quarter = RANK // NZ, levels // NY
        vmem = pl.BlockSpec(memory_space=pltpu.VMEM)
        dma = pltpu.SemaphoreType.DMA
        call = pl.pallas_call(
            lambda *refs: sweeps_kernel(points_all, levels_all, *refs),
            out_shape=(
                jax.ShapeDtypeStruct((RANK, points), F32),
                jax.ShapeDtypeStruct((RANK, levels), F32),
                jax.ShapeDtypeStruct((STEPS, RANK), F32),
            ),
            in_specs=[pl.BlockSpec(memory_space=pl.ANY), vmem, vmem],
            out_specs=(vmem, vmem, vmem),
            scratch_shapes=[
                pltpu.VMEM((steps, points, levels), BF16),
                pltpu.VMEM((steps, RANK, points), F32),
                pltpu.VMEM((steps, RANK, levels), F32),
                pltpu.VMEM((RANK, levels), BF16),
                pltpu.VMEM((RANK, points), BF16),
                pltpu.VMEM((RANK, levels), F32),
                pltpu.VMEM((RANK, points), F32),
                pltpu.VMEM((RANK, RANK), F32),
                pltpu.VMEM((RANK, RANK), F32),
                pltpu.VMEM((RANK, STEPS), F32),
                pltpu.VMEM((STEPS, RANK), F32),
                pltpu.VMEM((RANK, STEPS), F32),
                pltpu.VMEM((2, NX, RANK, share), F32),
                pltpu.VMEM((SWEEPS, NX, RANK, share), F32),
                pltpu.VMEM((SWEEPS, NX - 1, RANK, share), F32),
                pltpu.VMEM((SWEEPS, RANK, points), F32),
                pltpu.VMEM((32, 128), F32),
                pltpu.VMEM((SWEEPS, PTS_DEVICES, 16, 128), F32),
                pltpu.VMEM((SWEEPS, 32, 128), F32),
                pltpu.VMEM((NY, NZ, group, quarter), F32),
                pltpu.VMEM((SWEEPS, PTS_DEVICES, group, quarter), F32),
                pltpu.VMEM((SWEEPS, RANK, levels), F32),
                pltpu.VMEM((32, 128), F32),
                pltpu.VMEM((SWEEPS + 1, 32, 128), F32),
                pltpu.VMEM((SWEEPS + 1, NX, 32, 128), F32),
                pltpu.VMEM((8, 128), F32),
                pltpu.VMEM((SWEEPS, 8, 128), F32),
                pltpu.VMEM((SWEEPS, CHIPS, 8, 128), F32),
                dma((STEPS,)),
                dma((2 * NX,)),
                dma((SWEEPS,)),
                dma((SWEEPS, NX)),
                dma((SWEEPS, NX)),
                dma((SWEEPS, NX)),
                dma((SWEEPS,)),
                dma((SWEEPS,)),
                dma((SWEEPS,)),
                dma((SWEEPS,)),
                dma((SWEEPS + 1,)),
                dma((SWEEPS + 1, NX)),
                dma((SWEEPS,)),
                dma((SWEEPS,)),
            ],
            compiler_params=pltpu.CompilerParams(
                collective_id=0, has_side_effects=True, vmem_limit_bytes=48 * 2**20
            ),
            name="als_sweeps",
        )
        return call(tensor, level_init, time_init)

    return jax.shard_map(
        per_device,
        mesh=mesh,
        in_specs=(P(None, "pts", "var"), P(None, "var"), P()),
        out_specs=(P(None, "pts"), P(None, "var"), P()),
        check_vma=False,
    )
```

```python
import math

import jax
import jax.numpy as jnp
from jax import lax
from jax.experimental import pallas as pl
from jax.experimental.pallas import tpu as pltpu
from jax.sharding import PartitionSpec as P

RANK = 64
STEPS = 8
SWEEPS = 3
NY = NZ = NX = 4
PTS_DEVICES = NY * NZ
CHIPS = PTS_DEVICES * NX
EPSILON = 1e-06
F32 = jnp.float32
BF16 = jnp.bfloat16
HIGHEST = lax.Precision.HIGHEST
MESH = pl.DeviceIdType.MESH


def inverse_part(tiles, first, last, block=8):
    n = RANK
    shape = (8, n)
    row_ids = lax.broadcasted_iota(jnp.int32, shape, 0)
    lane_ids = lax.broadcasted_iota(jnp.int32, shape, 1)
    for start in range(first, last, block):
        panel = {
            j: [jnp.broadcast_to(tile[:, j : j + 1], shape) for tile in tiles]
            for j in range(start, start + block)
        }
        for k in range(start, start + block):
            t, s = divmod(k, 8)
            inv_pivot = 1.0 / jnp.broadcast_to(panel[k][t][s : s + 1, :], shape)
            col = list(panel[k])
            col[t] = jnp.where(row_ids == s, -1.0, col[t])
            for j in range(k + 1, start + block):
                scaled = jnp.broadcast_to(panel[j][t][s : s + 1, :], shape) * inv_pivot
                new = [panel[j][i] - col[i] * scaled for i in range(n // 8)]
                new[t] = jnp.where(row_ids == s, scaled, new[t])
                panel[j] = new
            row = jnp.broadcast_to(tiles[t][s : s + 1, :], shape) * inv_pivot
            row = jnp.where(lane_ids == k, inv_pivot, row)
            base = [jnp.where(lane_ids == k, 0.0, tile) for tile in tiles]
            base[t] = jnp.where(row_ids == s, 0.0, base[t])
            tiles = [base[i] - col[i] * row for i in range(n // 8)]
    return tiles


def row_tiles(matrix):
    return [matrix[8 * i : 8 * i + 8, :] for i in range(RANK // 8)]


def eye_mask():
    rows = lax.broadcasted_iota(jnp.int32, (RANK, RANK), 0)
    cols = lax.broadcasted_iota(jnp.int32, (RANK, RANK), 1)
    return rows == cols


def ridge_system(gram):
    eye = eye_mask()
    trace = jnp.sum(
        jnp.sum(jnp.where(eye, gram, 0.0), axis=0, keepdims=True), axis=1, keepdims=True
    )
    ridge = 0.01 * trace / RANK + EPSILON
    return gram + jnp.where(eye, ridge, 0.0)


def ridge_inverse(gram):
    return jnp.concatenate(inverse_part(row_tiles(ridge_system(gram)), 0, RANK), axis=0)


def split_gram(factor):
    high = factor.astype(BF16)
    low = (factor - high.astype(F32)).astype(BF16)
    both = jnp.concatenate([high, low], axis=0)
    return lax.dot_general(both, both, (((1,), (1,)), ((), ())), preferred_element_type=F32)


def folded(products):
    rows = products[:RANK] + products[RANK:]
    gram = rows[:, :RANK] + rows[:, RANK:]
    return jnp.concatenate([gram[:32], gram[32:]], axis=1)


def unpacked(packed):
    return jnp.concatenate([packed[:, :RANK], packed[:, RANK:]], axis=0)


def unit_scales(gram, count):
    diag = jnp.where(eye_mask(), gram, 0.0)
    col = 1.0 / jnp.sqrt(jnp.sum(diag, axis=1, keepdims=True) / count + EPSILON)
    row = 1.0 / jnp.sqrt(jnp.sum(diag, axis=0, keepdims=True) / count + EPSILON)
    return col, row


def sweeps_kernel(
    points_all,
    levels_all,
    x_hbm,
    level_hbm,
    time_hbm,
    point_out,
    level_out,
    time_out,
    x_ref,
    y_ref,
    y_sib,
    c_ref,
    lbf_ref,
    lu_ref,
    pu_ref,
    gl_ref,
    gp_ref,
    tt_ref,
    tr_ref,
    tp_ref,
    mp_half,
    sib_mp,
    line,
    m_full,
    g_send,
    g_recv,
    gh_full,
    ml_send,
    ml_recv,
    ml_full,
    inv_ref,
    gl_x,
    t_send,
    t_sib,
    t_all,
    load_sem,
    y_send_sem,
    line_send_sem,
    fw_send_sem,
    gl_send_sem,
    one_send_sem,
    y_sem,
    mp_sem,
    line_sem,
    fw_sem,
    g_sem,
    gs_sem,
    ml_sem,
    la_sem,
    glx_sem,
    ts_sem,
    ta_sem,
):
    pts, var = lax.axis_index("pts"), lax.axis_index("var")
    y, z = lax.div(pts, NZ), lax.rem(pts, NZ)
    x, core = lax.div(var, 2), lax.rem(var, 2)
    other = 1 - core
    sibling = (pts, x * 2 + other)
    chip = pts * NX + x
    xs = [lax.rem(x + d, NX) for d in range(NX)]
    ys = [lax.rem(y + d, NY) for d in range(NY)]
    zs = [lax.rem(z + d, NZ) for d in range(NZ)]
    var_peers = [
        (pts, xs[d] * 2 + c)
        for d, c in (
            (2, other),
            (2, core),
            (1, other),
            (3, other),
            (1, core),
            (3, core),
            (0, other),
        )
    ]
    x_devices = [(pts, xs[d] * 2 + core) for d in range(NX)]
    hops = (0, 1, 2, 1)
    pts_offsets = sorted(
        [(dy, dz) for dy in range(NY) for dz in range(NZ) if dy or dz],
        key=lambda o: -(hops[o[0]] + hops[o[1]]),
    )
    chip_offsets = sorted(
        [(dy, dz, dx) for dy in range(NY) for dz in range(NZ) for dx in range(NX) if dy or dz or dx],
        key=lambda o: -(hops[o[0]] + hops[o[1]] + hops[o[2]]),
    )

    def pts_device(dy, dz):
        return (ys[dy] * NZ + zs[dz], var)

    def chip_device(dy, dz, dx):
        return (ys[dy] * NZ + zs[dz], xs[dx] * 2 + core)

    def send(src, dst, send_sem, recv_sem, device):
        copy = pltpu.make_async_remote_copy(
            src_ref=src,
            dst_ref=dst,
            send_sem=send_sem,
            recv_sem=recv_sem,
            device_id=device,
            device_id_type=MESH,
        )
        copy.start()
        return copy

    def wait_bytes(ref, sem):
        pltpu.make_async_copy(ref, ref, sem).wait()

    level_load = pltpu.make_async_copy(level_hbm, lu_ref, load_sem.at[STEPS])
    time_load = pltpu.make_async_copy(time_hbm, tr_ref, load_sem.at[STEPS + 1])
    loads = [pltpu.make_async_copy(x_hbm.at[k], x_ref.at[k], load_sem.at[k]) for k in range(STEPS)]
    level_load.start()
    time_load.start()
    for load in loads:
        load.start()
    barrier = pltpu.get_barrier_semaphore()
    greeted = [pts_device(*offset) for offset in pts_offsets] + var_peers
    for device in greeted:
        pl.semaphore_signal(barrier, inc=1, device_id=device, device_id_type=MESH)

    half_points = y_ref.shape[3]
    share_points = half_points // NX
    quarter = c_ref.shape[2] // NY
    group = RANK // NZ

    def pass_levels(k):
        product = lax.dot_general(
            lbf_ref[...], x_ref[k], (((1,), (1,)), ((), ())), preferred_element_type=F32
        )
        y_ref[k, 0] = product[:, :half_points]
        y_ref[k, 1] = product[:, half_points:]

    def level_gram_copies(slot):
        view = gl_x.at[slot, var]
        return [
            pltpu.make_async_remote_copy(
                src_ref=view,
                dst_ref=view,
                send_sem=gl_send_sem.at[i],
                recv_sem=glx_sem.at[slot, i],
                device_id=device,
                device_id_type=MESH,
            )
            for i, device in enumerate(var_peers)
        ]

    def level_gram_start(slot, gram):
        gl_x[slot, var] = gram
        for copy in level_gram_copies(slot):
            copy.start()

    def level_gram_end(slot):
        for copy in level_gram_copies(slot):
            copy.wait()
        return unpacked(jnp.sum(gl_x[slot], axis=0))

    def column(values, k, lanes):
        return jnp.broadcast_to(values[:, k : k + 1], (values.shape[0], lanes))

    level_load.wait()
    lbf_ref[...] = lu_ref[...].astype(BF16)
    time_load.wait()
    tt_ref[...] = lax.dot_general(
        jnp.where(eye_mask(), 1.0, 0.0),
        tr_ref[...],
        (((1,), (1,)), ((), ())),
        precision=HIGHEST,
        preferred_element_type=F32,
    )
    for k in range(STEPS):
        loads[k].wait()
        pass_levels(k)
    first_cols = tt_ref[...]

    def first_half(c):
        total = column(first_cols, 0, half_points) * y_ref[0, c]
        for k in range(1, STEPS):
            total += column(first_cols, k, half_points) * y_ref[k, c]
        return total

    mp_half[...] = first_half(other)
    pl.semaphore_wait(barrier, len(greeted))
    to_sibling = send(mp_half, sib_mp, one_send_sem.at[0], mp_sem, sibling)
    level_gram_start(0, folded(split_gram(lu_ref[...])))
    own_half = first_half(core)
    to_sibling.wait()
    own_half += sib_mp[...]
    for j in range(NX):
        line[0, x, j] = own_half[:, j * share_points : (j + 1) * share_points]

    def sweep(s, carry):
        pieces = []
        for j in range(NX):
            view = line.at[s, x, j]
            pieces.append(
                [
                    send(view, view, line_send_sem.at[d, j], line_sem.at[s, d, j], x_devices[d])
                    for d in (2, 1, 3)
                ]
            )

        @pl.when(s == 0)
        def _():
            gl_ref[...] = level_gram_end(0)

        time_cols = tt_ref[...]
        rows = tr_ref[...]
        time_gram = column(time_cols, 0, RANK) * rows[0:1, :]
        for k in range(1, STEPS):
            time_gram += column(time_cols, k, RANK) * rows[k : k + 1, :]
        inverse = ridge_inverse(gl_ref[...] * time_gram)
        inv_ref[...] = inverse

        forward = []

        def arrive(j):
            for copy in pieces[j]:
                copy.wait()
            total = line[s, 0, j]
            for i in range(1, NX):
                total += line[s, i, j]
            m_full[s, j, core] = total
            view = m_full.at[s, j, core]
            forward.append(send(view, view, fw_send_sem.at[j], fw_sem.at[s, j], sibling))

        def solve_points(j):
            forward[j].wait()
            sums = jnp.concatenate([m_full[s, j, 0], m_full[s, j, 1]], axis=1)
            solved = jnp.dot(inverse, sums, precision=HIGHEST, preferred_element_type=F32)
            starts = [c * half_points + j * share_points for c in range(2)]
            for i, start in enumerate(starts):
                pu_ref[:, start : start + share_points] = solved[
                    :, i * share_points : (i + 1) * share_points
                ]
            return solved.astype(BF16), starts

        def block(k, starts, lanes):
            return jnp.concatenate(
                [x_ref[k, start : start + share_points, lanes] for start in starts], axis=0
            )

        arrive(0)
        for j in range(NX - 1):
            arrive(j + 1)
            factor, starts = solve_points(j)
            for k in range(STEPS):
                product = jnp.dot(
                    factor, block(k, starts, slice(None)), preferred_element_type=F32
                )
                c_ref[k] = c_ref[k] + product if j else product
        factor, starts = solve_points(NX - 1)

        spread = [column(time_cols, k, quarter) for k in range(STEPS)]
        for dy in (2, 1, 3, 0):
            q = ys[dy]
            lanes = pl.ds(pl.multiple_of(q * quarter, quarter), quarter)
            total = None
            for k in range(STEPS):
                product = c_ref[k, :, lanes] + jnp.dot(
                    factor, block(k, starts, lanes), preferred_element_type=F32
                )
                c_ref[k, :, lanes] = product
                term = spread[k] * product
                total = term if total is None else total + term
            for j in range(NZ):
                ml_send[q, j] = total[j * group : (j + 1) * group]
            for dz in (2, 1, 3, 0):
                if dy or dz:
                    send(
                        ml_send.at[q, zs[dz]],
                        ml_recv.at[s, pts],
                        one_send_sem.at[1],
                        ml_sem.at[s],
                        pts_device(dy, dz),
                    )
        ml_recv[s, pts] = ml_send[y, z]

        g_send[...] = folded(split_gram(pu_ref[...]))
        half = pl.ds(pl.multiple_of(core * 16, 16), 16)
        g_recv[s, pts] = g_send[half, :]
        for offset in pts_offsets:
            send(
                g_send.at[half, :],
                g_recv.at[s, pts],
                one_send_sem.at[2],
                g_sem.at[s],
                pts_device(*offset),
            )

        others = pl.ds(0, PTS_DEVICES - 1)
        wait_bytes(ml_recv.at[s, others], ml_sem.at[s])
        wait_bytes(ml_recv.at[s, others], one_send_sem.at[1])
        own_rows = pl.ds(pl.multiple_of(z * group, group), group)
        own_cols = pl.ds(pl.multiple_of(y * quarter, quarter), quarter)
        ml_full[s, own_rows, own_cols] = jnp.sum(ml_recv[s], axis=0)
        level_view = ml_full.at[s, own_rows, own_cols]
        for dy, dz in sorted(pts_offsets, key=lambda o: (hops[o[0]], -hops[o[1]])):
            send(
                level_view, level_view, one_send_sem.at[1], la_sem.at[s, dy], pts_device(dy, dz)
            )

        wait_bytes(g_recv.at[s, others], g_sem.at[s])
        wait_bytes(g_recv.at[s, others], one_send_sem.at[2])
        gh_full[s, half, :] = jnp.sum(g_recv[s], axis=0)
        half_view = gh_full.at[s, half, :]
        half_copy = send(half_view, half_view, one_send_sem.at[3], gs_sem.at[s], sibling)
        half_copy.wait()
        raw_gram = unpacked(gh_full[s])
        point_col, point_row = unit_scales(raw_gram, points_all)
        point_gram = point_col * raw_gram * point_row
        gp_ref[...] = point_gram
        inverse = ridge_inverse(point_gram * time_gram) * point_row
        point_out[...] = pu_ref[...] * point_col

        level_products = jnp.zeros((2 * RANK, 2 * RANK), F32)
        for dy in (0, 1, 3, 2):
            count = NZ if dy else NZ - 1
            wait_bytes(ml_recv.at[s, pl.ds(0, count)], la_sem.at[s, dy])
            start = pl.multiple_of(ys[(NY - dy) % NY] * quarter, quarter)
            lanes = pl.ds(start, quarter)
            solved = jnp.dot(
                inverse, ml_full[s, :, lanes], precision=HIGHEST, preferred_element_type=F32
            )
            lu_ref[:, lanes] = solved
            lbf_ref[:, lanes] = solved.astype(BF16)
            level_products += split_gram(solved)
            if dy == 2:
                level_gram_start(s + 1, folded(level_products))
            scaled = solved * point_col
            for k in range(STEPS):
                product = c_ref[k, :, lanes] * scaled
                part = product[:, :128]
                for i in range(128, quarter, 128):
                    part += product[:, i : i + 128]
                tp_ref[k] = tp_ref[k] + part if dy else part
        lane_ids = lax.broadcasted_iota(jnp.int32, (RANK, 128), 1)
        products = jnp.zeros((RANK, 128), F32)
        for k in range(STEPS):
            sums = jnp.sum(tp_ref[k], axis=1, keepdims=True)
            products = jnp.where(lane_ids == k, sums, products)
        t_rows = jnp.transpose(products)[:STEPS]
        t_send[...] = jnp.concatenate([t_rows[:4], t_rows[4:]], axis=1)
        time_copy = send(t_send, t_sib.at[s], one_send_sem.at[4], ts_sem.at[s], sibling)
        wait_bytes(ml_recv.at[s, others], one_send_sem.at[1])
        time_copy.wait()
        t_all[s, chip] = t_send[...] + t_sib[s]
        time_view = t_all.at[s, chip]
        for offset in chip_offsets:
            send(time_view, time_view, one_send_sem.at[5], ta_sem.at[s], chip_device(*offset))

        y_copies = []

        def next_products(first, last):
            for k in range(first, last):
                pass_levels(k)
            for k in range(first, last):
                half_view = y_ref.at[k, other]
                y_copies.append(
                    send(half_view, y_sib.at[s, k], y_send_sem.at[k], y_sem.at[s, k], sibling)
                )

        next_products(0, 2)
        next_products(2, 4)
        raw_gram = level_gram_end(s + 1)
        level_col, level_row = unit_scales(raw_gram, levels_all)
        level_gram = level_col * raw_gram * level_row
        gl_ref[...] = level_gram
        tiles = inverse_part(row_tiles(ridge_system(gp_ref[...] * level_gram)), 0, RANK // 2)
        inv_ref[...] = jnp.concatenate(tiles, axis=0)
        next_products(4, 6)
        tiles = inverse_part(row_tiles(inv_ref[...]), RANK // 2, RANK)
        inverse = jnp.concatenate(tiles, axis=0)
        inv_ref[...] = inverse
        level_out[...] = lu_ref[...] * level_col
        next_products(6, 8)
        chips = pl.ds(0, CHIPS - 1)
        wait_bytes(t_all.at[s, chips], ta_sem.at[s])
        wait_bytes(t_all.at[s, chips], one_send_sem.at[5])
        mttk_time = unpacked(jnp.sum(t_all[s], axis=0)) * level_row
        tr_ref[...] = jnp.dot(mttk_time, inverse, precision=HIGHEST, preferred_element_type=F32)
        next_cols = lax.dot_general(
            inverse,
            mttk_time,
            (((1,), (1,)), ((), ())),
            precision=HIGHEST,
            preferred_element_type=F32,
        )
        tt_ref[...] = next_cols
        for copy in y_copies:
            copy.wait()

        @pl.when(s < SWEEPS - 1)
        def _():
            weights = next_cols * level_col
            for j in range(NX):
                lanes = slice(j * share_points, (j + 1) * share_points)
                total = None
                for k in range(STEPS):
                    both = y_ref[k, core, :, lanes] + y_sib[s, k, :, lanes]
                    term = column(weights, k, share_points) * both
                    total = term if total is None else total + term
                line[s + 1, x, j] = total

        return carry

    lax.fori_loop(0, SWEEPS, sweep, 0)
    time_out[...] = tr_ref[...] * math.sqrt(points_all * levels_all)


def hand_over(point_in, level_in, time_in, point_out, level_out, time_out):
    point_out[...] = point_in[...]
    level_out[...] = level_in[...]
    time_out[...] = time_in[...]


def solution(mesh):
    def per_device(tensor, level_init, time_init):
        steps, points, levels = tensor.shape
        points_all = points * mesh.shape["pts"]
        levels_all = levels * mesh.shape["var"]
        share = points // (2 * NX)
        group, quarter = RANK // NZ, levels // NY
        anywhere = pl.BlockSpec(memory_space=pl.ANY)
        vmem = pl.BlockSpec(memory_space=pltpu.VMEM)
        dma = pltpu.SemaphoreType.DMA
        outputs = (
            jax.ShapeDtypeStruct((RANK, points), F32),
            jax.ShapeDtypeStruct((RANK, levels), F32),
            jax.ShapeDtypeStruct((STEPS, RANK), F32),
        )
        call = pl.pallas_call(
            lambda *refs: sweeps_kernel(points_all, levels_all, *refs),
            out_shape=outputs,
            in_specs=[anywhere, anywhere, anywhere],
            out_specs=(vmem, vmem, vmem),
            scratch_shapes=[
                pltpu.VMEM((steps, points, levels), BF16),
                pltpu.VMEM((steps, 2, RANK, points // 2), F32),
                pltpu.VMEM((SWEEPS, steps, RANK, points // 2), F32),
                pltpu.VMEM((steps, RANK, levels), F32),
                pltpu.VMEM((RANK, levels), BF16),
                pltpu.VMEM((RANK, levels), F32),
                pltpu.VMEM((RANK, points), F32),
                pltpu.VMEM((RANK, RANK), F32),
                pltpu.VMEM((RANK, RANK), F32),
                pltpu.VMEM((RANK, STEPS), F32),
                pltpu.VMEM((STEPS, RANK), F32),
                pltpu.VMEM((STEPS, RANK, 128), F32),
                pltpu.VMEM((RANK, points // 2), F32),
                pltpu.VMEM((RANK, points // 2), F32),
                pltpu.VMEM((SWEEPS, NX, NX, RANK, share), F32),
                pltpu.VMEM((SWEEPS, NX, 2, RANK, share), F32),
                pltpu.VMEM((32, 128), F32),
                pltpu.VMEM((SWEEPS, PTS_DEVICES, 16, 128), F32),
                pltpu.VMEM((SWEEPS, 32, 128), F32),
                pltpu.VMEM((NY, NZ, group, quarter), F32),
                pltpu.VMEM((SWEEPS, PTS_DEVICES, group, quarter), F32),
                pltpu.VMEM((SWEEPS, RANK, levels), F32),
                pltpu.VMEM((RANK, RANK), F32),
                pltpu.VMEM((SWEEPS + 1, 2 * NX, 32, 128), F32),
                pltpu.VMEM((4, 128), F32),
                pltpu.VMEM((SWEEPS, 4, 128), F32),
                pltpu.VMEM((SWEEPS, CHIPS, 4, 128), F32),
                dma((STEPS + 2,)),
                dma((STEPS,)),
                dma((NX, NX)),
                dma((NX,)),
                dma((2 * NX - 1,)),
                dma((6,)),
                dma((SWEEPS, STEPS)),
                dma,
                dma((SWEEPS, NX, NX)),
                dma((SWEEPS, NX)),
                dma((SWEEPS,)),
                dma((SWEEPS,)),
                dma((SWEEPS,)),
                dma((SWEEPS, NY)),
                dma((SWEEPS + 1, 2 * NX - 1)),
                dma((SWEEPS,)),
                dma((SWEEPS,)),
            ],
            compiler_params=pltpu.CompilerParams(
                collective_id=0, has_side_effects=True, vmem_limit_bytes=63 * 2**20
            ),
            name="als_sweeps",
        )
        results = call(tensor, level_init, time_init)
        return pl.pallas_call(
            hand_over,
            out_shape=outputs,
            in_specs=[vmem, vmem, vmem],
            out_specs=(vmem, vmem, vmem),
            name="hand_over",
        )(*results)

    return jax.shard_map(
        per_device,
        mesh=mesh,
        in_specs=(P(None, "pts", "var"), P(None, "var"), P()),
        out_specs=(P(None, "pts"), P(None, "var"), P()),
        check_vma=False,
    )
```

```python
import math

import jax
import jax.numpy as jnp
from jax import lax
from jax.experimental import pallas as pl
from jax.experimental.pallas import tpu as pltpu
from jax.sharding import PartitionSpec as P

RANK = 64
STEPS = 8
SWEEPS = 3
NY = NZ = NX = 4
PTS_DEVICES = NY * NZ
CHIPS = PTS_DEVICES * NX
EPSILON = 1e-06
F32 = jnp.float32
BF16 = jnp.bfloat16
HIGHEST = lax.Precision.HIGHEST
MESH = pl.DeviceIdType.MESH


def inverse_part(tiles, first, last, block=8):
    n = RANK
    shape = (8, n)
    row_ids = lax.broadcasted_iota(jnp.int32, shape, 0)
    lane_ids = lax.broadcasted_iota(jnp.int32, shape, 1)
    for start in range(first, last, block):
        panel = {
            j: [jnp.broadcast_to(tile[:, j : j + 1], shape) for tile in tiles]
            for j in range(start, start + block)
        }
        for k in range(start, start + block):
            t, s = divmod(k, 8)
            inv_pivot = 1.0 / jnp.broadcast_to(panel[k][t][s : s + 1, :], shape)
            col = list(panel[k])
            col[t] = jnp.where(row_ids == s, -1.0, col[t])
            for j in range(k + 1, start + block):
                scaled = jnp.broadcast_to(panel[j][t][s : s + 1, :], shape) * inv_pivot
                new = [panel[j][i] - col[i] * scaled for i in range(n // 8)]
                new[t] = jnp.where(row_ids == s, scaled, new[t])
                panel[j] = new
            row = jnp.broadcast_to(tiles[t][s : s + 1, :], shape) * inv_pivot
            row = jnp.where(lane_ids == k, inv_pivot, row)
            base = [jnp.where(lane_ids == k, 0.0, tile) for tile in tiles]
            base[t] = jnp.where(row_ids == s, 0.0, base[t])
            tiles = [base[i] - col[i] * row for i in range(n // 8)]
    return tiles


def row_tiles(matrix):
    return [matrix[8 * i : 8 * i + 8, :] for i in range(RANK // 8)]


def eye_mask():
    rows = lax.broadcasted_iota(jnp.int32, (RANK, RANK), 0)
    cols = lax.broadcasted_iota(jnp.int32, (RANK, RANK), 1)
    return rows == cols


def ridge_system(gram):
    eye = eye_mask()
    trace = jnp.sum(
        jnp.sum(jnp.where(eye, gram, 0.0), axis=0, keepdims=True), axis=1, keepdims=True
    )
    ridge = 0.01 * trace / RANK + EPSILON
    return gram + jnp.where(eye, ridge, 0.0)


def ridge_inverse(gram):
    return jnp.concatenate(inverse_part(row_tiles(ridge_system(gram)), 0, RANK), axis=0)


def split_gram(factor):
    high = factor.astype(BF16)
    low = (factor - high.astype(F32)).astype(BF16)
    both = jnp.concatenate([high, low], axis=0)
    return lax.dot_general(both, both, (((1,), (1,)), ((), ())), preferred_element_type=F32)


def folded(products):
    rows = products[:RANK] + products[RANK:]
    gram = rows[:, :RANK] + rows[:, RANK:]
    return jnp.concatenate([gram[:32], gram[32:]], axis=1)


def unpacked(packed):
    return jnp.concatenate([packed[:, :RANK], packed[:, RANK:]], axis=0)


def unit_scales(gram, count):
    diag = jnp.where(eye_mask(), gram, 0.0)
    col = 1.0 / jnp.sqrt(jnp.sum(diag, axis=1, keepdims=True) / count + EPSILON)
    row = 1.0 / jnp.sqrt(jnp.sum(diag, axis=0, keepdims=True) / count + EPSILON)
    return col, row


def sweeps_kernel(
    points_all,
    levels_all,
    x_hbm,
    level_hbm,
    time_hbm,
    point_out,
    level_out,
    time_out,
    x_ref,
    y_ref,
    y_sib,
    c_ref,
    lbf_ref,
    lu_ref,
    pu_ref,
    gl_ref,
    gp_ref,
    tt_ref,
    tr_ref,
    tp_ref,
    mp_half,
    sib_mp,
    line,
    m_full,
    g_send,
    g_recv,
    gh_full,
    ml_send,
    ml_recv,
    ml_full,
    inv_ref,
    gl_x,
    t_send,
    t_sib,
    t_all,
    load_sem,
    y_send_sem,
    line_send_sem,
    fw_send_sem,
    gl_send_sem,
    one_send_sem,
    y_sem,
    mp_sem,
    line_sem,
    fw_sem,
    g_sem,
    gs_sem,
    ml_sem,
    la_sem,
    glx_sem,
    ts_sem,
    ta_sem,
):
    pts, var = lax.axis_index("pts"), lax.axis_index("var")
    y, z = lax.div(pts, NZ), lax.rem(pts, NZ)
    x, core = lax.div(var, 2), lax.rem(var, 2)
    other = 1 - core
    sibling = (pts, x * 2 + other)
    chip = pts * NX + x
    xs = [lax.rem(x + d, NX) for d in range(NX)]
    ys = [lax.rem(y + d, NY) for d in range(NY)]
    zs = [lax.rem(z + d, NZ) for d in range(NZ)]
    var_peers = [
        (pts, xs[d] * 2 + c)
        for d, c in (
            (2, other),
            (2, core),
            (1, other),
            (3, other),
            (1, core),
            (3, core),
            (0, other),
        )
    ]
    x_devices = [(pts, xs[d] * 2 + core) for d in range(NX)]
    hops = (0, 1, 2, 1)
    pts_offsets = sorted(
        [(dy, dz) for dy in range(NY) for dz in range(NZ) if dy or dz],
        key=lambda o: -(hops[o[0]] + hops[o[1]]),
    )
    chip_offsets = sorted(
        [(dy, dz, dx) for dy in range(NY) for dz in range(NZ) for dx in range(NX) if dy or dz or dx],
        key=lambda o: -(hops[o[0]] + hops[o[1]] + hops[o[2]]),
    )

    def pts_device(dy, dz):
        return (ys[dy] * NZ + zs[dz], var)

    def chip_device(dy, dz, dx):
        return (ys[dy] * NZ + zs[dz], xs[dx] * 2 + core)

    def send(src, dst, send_sem, recv_sem, device):
        copy = pltpu.make_async_remote_copy(
            src_ref=src,
            dst_ref=dst,
            send_sem=send_sem,
            recv_sem=recv_sem,
            device_id=device,
            device_id_type=MESH,
        )
        copy.start()
        return copy

    def wait_bytes(ref, sem):
        pltpu.make_async_copy(ref, ref, sem).wait()

    barrier = pltpu.get_barrier_semaphore()
    greeted = [pts_device(*offset) for offset in pts_offsets] + var_peers
    for device in greeted:
        pl.semaphore_signal(barrier, inc=1, device_id=device, device_id_type=MESH)
    level_load = pltpu.make_async_copy(level_hbm, lu_ref, load_sem.at[STEPS])
    time_load = pltpu.make_async_copy(time_hbm, tr_ref, load_sem.at[STEPS + 1])
    loads = [pltpu.make_async_copy(x_hbm.at[k], x_ref.at[k], load_sem.at[k]) for k in range(STEPS)]
    level_load.start()
    time_load.start()
    for load in loads:
        load.start()

    half_points = y_ref.shape[3]
    share_points = half_points // NX
    quarter = c_ref.shape[2] // NY
    group = RANK // NZ

    def pass_levels(k):
        product = lax.dot_general(
            lbf_ref[...], x_ref[k], (((1,), (1,)), ((), ())), preferred_element_type=F32
        )
        y_ref[k, 0] = product[:, :half_points]
        y_ref[k, 1] = product[:, half_points:]

    def level_gram_copies(slot):
        view = gl_x.at[slot, var]
        return [
            pltpu.make_async_remote_copy(
                src_ref=view,
                dst_ref=view,
                send_sem=gl_send_sem.at[i],
                recv_sem=glx_sem.at[slot, i],
                device_id=device,
                device_id_type=MESH,
            )
            for i, device in enumerate(var_peers)
        ]

    def level_gram_start(slot, gram):
        gl_x[slot, var] = gram
        for copy in level_gram_copies(slot):
            copy.start()

    def level_gram_end(slot):
        for copy in level_gram_copies(slot):
            copy.wait()
        return unpacked(jnp.sum(gl_x[slot], axis=0))

    def column(values, k, lanes):
        return jnp.broadcast_to(values[:, k : k + 1], (values.shape[0], lanes))

    def piece_copies(s, j):
        view = line.at[s, x, j]
        return [
            pltpu.make_async_remote_copy(
                src_ref=view,
                dst_ref=view,
                send_sem=line_send_sem.at[d, j],
                recv_sem=line_sem.at[s, d, j],
                device_id=x_devices[d],
                device_id_type=MESH,
            )
            for d in (2, 1, 3)
        ]

    level_load.wait()
    lbf_ref[...] = lu_ref[...].astype(BF16)
    time_load.wait()
    tt_ref[...] = lax.dot_general(
        jnp.where(eye_mask(), 1.0, 0.0),
        tr_ref[...],
        (((1,), (1,)), ((), ())),
        precision=HIGHEST,
        preferred_element_type=F32,
    )
    for k in range(STEPS):
        loads[k].wait()
        pass_levels(k)
    first_cols = tt_ref[...]

    def first_half(c):
        total = column(first_cols, 0, half_points) * y_ref[0, c]
        for k in range(1, STEPS):
            total += column(first_cols, k, half_points) * y_ref[k, c]
        return total

    mp_half[...] = first_half(other)
    pl.semaphore_wait(barrier, len(greeted))
    to_sibling = send(mp_half, sib_mp, one_send_sem.at[0], mp_sem, sibling)
    level_gram_start(0, folded(split_gram(lu_ref[...])))
    own_half = first_half(core)
    to_sibling.wait()
    own_half += sib_mp[...]
    for j in range(NX):
        line[0, x, j] = own_half[:, j * share_points : (j + 1) * share_points]
        for copy in piece_copies(0, j):
            copy.start()

    def sweep(s, carry):
        pieces = [piece_copies(s, j) for j in range(NX)]

        @pl.when(s == 0)
        def _():
            gl_ref[...] = level_gram_end(0)

        time_cols = tt_ref[...]
        rows = tr_ref[...]
        time_gram = column(time_cols, 0, RANK) * rows[0:1, :]
        for k in range(1, STEPS):
            time_gram += column(time_cols, k, RANK) * rows[k : k + 1, :]
        inverse = ridge_inverse(gl_ref[...] * time_gram)
        inv_ref[...] = inverse

        forward = []

        def arrive(j):
            for copy in pieces[j]:
                copy.wait()
            total = line[s, 0, j]
            for i in range(1, NX):
                total += line[s, i, j]
            m_full[s, j, core] = total
            view = m_full.at[s, j, core]
            forward.append(send(view, view, fw_send_sem.at[j], fw_sem.at[s, j], sibling))

        def solve_points(j):
            forward[j].wait()
            sums = jnp.concatenate([m_full[s, j, 0], m_full[s, j, 1]], axis=1)
            solved = jnp.dot(inverse, sums, precision=HIGHEST, preferred_element_type=F32)
            starts = [c * half_points + j * share_points for c in range(2)]
            for i, start in enumerate(starts):
                pu_ref[:, start : start + share_points] = solved[
                    :, i * share_points : (i + 1) * share_points
                ]
            return solved.astype(BF16), starts

        def block(k, starts, lanes):
            return jnp.concatenate(
                [x_ref[k, start : start + share_points, lanes] for start in starts], axis=0
            )

        arrive(0)
        for j in range(NX - 1):
            arrive(j + 1)
            factor, starts = solve_points(j)
            for k in range(STEPS):
                product = jnp.dot(
                    factor, block(k, starts, slice(None)), preferred_element_type=F32
                )
                c_ref[k] = c_ref[k] + product if j else product
        factor, starts = solve_points(NX - 1)

        spread = [column(time_cols, k, quarter) for k in range(STEPS)]
        for dy in (2, 1, 3, 0):
            q = ys[dy]
            lanes = pl.ds(pl.multiple_of(q * quarter, quarter), quarter)
            total = None
            for k in range(STEPS):
                product = c_ref[k, :, lanes] + jnp.dot(
                    factor, block(k, starts, lanes), preferred_element_type=F32
                )
                c_ref[k, :, lanes] = product
                term = spread[k] * product
                total = term if total is None else total + term
            for j in range(NZ):
                ml_send[q, j] = total[j * group : (j + 1) * group]
            for dz in (2, 1, 3, 0):
                if dy or dz:
                    send(
                        ml_send.at[q, zs[dz]],
                        ml_recv.at[s, pts],
                        one_send_sem.at[1],
                        ml_sem.at[s],
                        pts_device(dy, dz),
                    )
        ml_recv[s, pts] = ml_send[y, z]

        g_send[...] = folded(split_gram(pu_ref[...]))
        half = pl.ds(pl.multiple_of(core * 16, 16), 16)
        g_recv[s, pts] = g_send[half, :]
        for offset in pts_offsets:
            send(
                g_send.at[half, :],
                g_recv.at[s, pts],
                one_send_sem.at[2],
                g_sem.at[s],
                pts_device(*offset),
            )

        others = pl.ds(0, PTS_DEVICES - 1)
        wait_bytes(ml_recv.at[s, others], ml_sem.at[s])
        own_rows = pl.ds(pl.multiple_of(z * group, group), group)
        own_cols = pl.ds(pl.multiple_of(y * quarter, quarter), quarter)
        ml_full[s, own_rows, own_cols] = jnp.sum(ml_recv[s], axis=0)
        level_view = ml_full.at[s, own_rows, own_cols]
        wait_bytes(ml_recv.at[s, others], one_send_sem.at[1])
        for dy, dz in sorted(pts_offsets, key=lambda o: (hops[o[0]], -hops[o[1]])):
            send(
                level_view, level_view, one_send_sem.at[1], la_sem.at[s, dy], pts_device(dy, dz)
            )

        wait_bytes(g_recv.at[s, others], g_sem.at[s])
        wait_bytes(g_recv.at[s, others], one_send_sem.at[2])
        gh_full[s, half, :] = jnp.sum(g_recv[s], axis=0)
        half_view = gh_full.at[s, half, :]
        half_copy = send(half_view, half_view, one_send_sem.at[3], gs_sem.at[s], sibling)
        half_copy.wait()
        raw_gram = unpacked(gh_full[s])
        point_col, point_row = unit_scales(raw_gram, points_all)
        point_gram = point_col * raw_gram * point_row
        gp_ref[...] = point_gram
        inverse = ridge_inverse(point_gram * time_gram) * point_row
        point_out[...] = pu_ref[...] * point_col

        level_products = jnp.zeros((2 * RANK, 2 * RANK), F32)
        for dy in (0, 1, 3, 2):
            count = NZ if dy else NZ - 1
            wait_bytes(ml_recv.at[s, pl.ds(0, count)], la_sem.at[s, dy])
            start = pl.multiple_of(ys[(NY - dy) % NY] * quarter, quarter)
            lanes = pl.ds(start, quarter)
            solved = jnp.dot(
                inverse, ml_full[s, :, lanes], precision=HIGHEST, preferred_element_type=F32
            )
            lu_ref[:, lanes] = solved
            lbf_ref[:, lanes] = solved.astype(BF16)
            level_products += split_gram(solved)
            if dy == 2:
                level_gram_start(s + 1, folded(level_products))
            scaled = solved * point_col
            for k in range(STEPS):
                product = c_ref[k, :, lanes] * scaled
                part = product[:, :128]
                for i in range(128, quarter, 128):
                    part += product[:, i : i + 128]
                tp_ref[k] = tp_ref[k] + part if dy else part
        lane_ids = lax.broadcasted_iota(jnp.int32, (RANK, 128), 1)
        products = jnp.zeros((RANK, 128), F32)
        for k in range(STEPS):
            sums = jnp.sum(tp_ref[k], axis=1, keepdims=True)
            products = jnp.where(lane_ids == k, sums, products)
        t_rows = jnp.transpose(products)[:STEPS]
        t_send[...] = jnp.concatenate([t_rows[:4], t_rows[4:]], axis=1)
        time_copy = send(t_send, t_sib.at[s], one_send_sem.at[4], ts_sem.at[s], sibling)
        wait_bytes(ml_recv.at[s, others], one_send_sem.at[1])
        time_copy.wait()
        t_all[s, chip] = t_send[...] + t_sib[s]
        time_view = t_all.at[s, chip]
        for offset in chip_offsets:
            send(time_view, time_view, one_send_sem.at[5], ta_sem.at[s], chip_device(*offset))

        y_copies = []

        def next_products(first, last):
            for k in range(first, last):
                pass_levels(k)
            for k in range(first, last):
                half_view = y_ref.at[k, other]
                y_copies.append(
                    send(half_view, y_sib.at[s, k], y_send_sem.at[k], y_sem.at[s, k], sibling)
                )

        next_products(0, 2)
        next_products(2, 4)
        raw_gram = level_gram_end(s + 1)
        level_col, level_row = unit_scales(raw_gram, levels_all)
        level_gram = level_col * raw_gram * level_row
        gl_ref[...] = level_gram
        tiles = inverse_part(row_tiles(ridge_system(gp_ref[...] * level_gram)), 0, RANK // 2)
        inv_ref[...] = jnp.concatenate(tiles, axis=0)
        next_products(4, 6)
        tiles = inverse_part(row_tiles(inv_ref[...]), RANK // 2, RANK)
        inverse = jnp.concatenate(tiles, axis=0)
        inv_ref[...] = inverse
        level_out[...] = lu_ref[...] * level_col
        next_products(6, 8)
        chips = pl.ds(0, CHIPS - 1)
        wait_bytes(t_all.at[s, chips], ta_sem.at[s])
        wait_bytes(t_all.at[s, chips], one_send_sem.at[5])
        mttk_time = unpacked(jnp.sum(t_all[s], axis=0)) * level_row
        tr_ref[...] = jnp.dot(mttk_time, inverse, precision=HIGHEST, preferred_element_type=F32)
        next_cols = lax.dot_general(
            inverse,
            mttk_time,
            (((1,), (1,)), ((), ())),
            precision=HIGHEST,
            preferred_element_type=F32,
        )
        tt_ref[...] = next_cols
        for copy in y_copies:
            copy.wait()

        @pl.when(s < SWEEPS - 1)
        def _():
            weights = next_cols * level_col
            for j in range(NX):
                lanes = slice(j * share_points, (j + 1) * share_points)
                total = None
                for k in range(STEPS):
                    both = y_ref[k, core, :, lanes] + y_sib[s, k, :, lanes]
                    term = column(weights, k, share_points) * both
                    total = term if total is None else total + term
                line[s + 1, x, j] = total
                for copy in piece_copies(s + 1, j):
                    copy.start()

        return carry

    lax.fori_loop(0, SWEEPS, sweep, 0)
    time_out[...] = tr_ref[...] * math.sqrt(points_all * levels_all)


def hand_over(point_in, level_in, time_in, point_out, level_out, time_out):
    point_out[...] = point_in[...]
    level_out[...] = level_in[...]
    time_out[...] = time_in[...]


def solution(mesh):
    def per_device(tensor, level_init, time_init):
        steps, points, levels = tensor.shape
        points_all = points * mesh.shape["pts"]
        levels_all = levels * mesh.shape["var"]
        share = points // (2 * NX)
        group, quarter = RANK // NZ, levels // NY
        anywhere = pl.BlockSpec(memory_space=pl.ANY)
        vmem = pl.BlockSpec(memory_space=pltpu.VMEM)
        dma = pltpu.SemaphoreType.DMA
        outputs = (
            jax.ShapeDtypeStruct((RANK, points), F32),
            jax.ShapeDtypeStruct((RANK, levels), F32),
            jax.ShapeDtypeStruct((STEPS, RANK), F32),
        )
        call = pl.pallas_call(
            lambda *refs: sweeps_kernel(points_all, levels_all, *refs),
            out_shape=outputs,
            in_specs=[anywhere, anywhere, anywhere],
            out_specs=(vmem, vmem, vmem),
            scratch_shapes=[
                pltpu.VMEM((steps, points, levels), BF16),
                pltpu.VMEM((steps, 2, RANK, points // 2), F32),
                pltpu.VMEM((SWEEPS, steps, RANK, points // 2), F32),
                pltpu.VMEM((steps, RANK, levels), F32),
                pltpu.VMEM((RANK, levels), BF16),
                pltpu.VMEM((RANK, levels), F32),
                pltpu.VMEM((RANK, points), F32),
                pltpu.VMEM((RANK, RANK), F32),
                pltpu.VMEM((RANK, RANK), F32),
                pltpu.VMEM((RANK, STEPS), F32),
                pltpu.VMEM((STEPS, RANK), F32),
                pltpu.VMEM((STEPS, RANK, 128), F32),
                pltpu.VMEM((RANK, points // 2), F32),
                pltpu.VMEM((RANK, points // 2), F32),
                pltpu.VMEM((SWEEPS, NX, NX, RANK, share), F32),
                pltpu.VMEM((SWEEPS, NX, 2, RANK, share), F32),
                pltpu.VMEM((32, 128), F32),
                pltpu.VMEM((SWEEPS, PTS_DEVICES, 16, 128), F32),
                pltpu.VMEM((SWEEPS, 32, 128), F32),
                pltpu.VMEM((NY, NZ, group, quarter), F32),
                pltpu.VMEM((SWEEPS, PTS_DEVICES, group, quarter), F32),
                pltpu.VMEM((SWEEPS, RANK, levels), F32),
                pltpu.VMEM((RANK, RANK), F32),
                pltpu.VMEM((SWEEPS + 1, 2 * NX, 32, 128), F32),
                pltpu.VMEM((4, 128), F32),
                pltpu.VMEM((SWEEPS, 4, 128), F32),
                pltpu.VMEM((SWEEPS, CHIPS, 4, 128), F32),
                dma((STEPS + 2,)),
                dma((STEPS,)),
                dma((NX, NX)),
                dma((NX,)),
                dma((2 * NX - 1,)),
                dma((6,)),
                dma((SWEEPS, STEPS)),
                dma,
                dma((SWEEPS, NX, NX)),
                dma((SWEEPS, NX)),
                dma((SWEEPS,)),
                dma((SWEEPS,)),
                dma((SWEEPS,)),
                dma((SWEEPS, NY)),
                dma((SWEEPS + 1, 2 * NX - 1)),
                dma((SWEEPS,)),
                dma((SWEEPS,)),
            ],
            compiler_params=pltpu.CompilerParams(
                collective_id=0, has_side_effects=True, vmem_limit_bytes=63 * 2**20
            ),
            name="als_sweeps",
        )
        results = call(tensor, level_init, time_init)
        return pl.pallas_call(
            hand_over,
            out_shape=outputs,
            in_specs=[vmem, vmem, vmem],
            out_specs=(vmem, vmem, vmem),
            name="hand_over",
        )(*results)

    return jax.shard_map(
        per_device,
        mesh=mesh,
        in_specs=(P(None, "pts", "var"), P(None, "var"), P()),
        out_specs=(P(None, "pts"), P(None, "var"), P()),
        check_vma=False,
    )
```
